256 devices in a mesh: context: 32 (over x, z_hi, y), tensor: 8 (over z_lo, core).
Axes of the slice: x: 4, y: 4, z: 8 (z_hi: 2, z_lo: 4; z = z_hi * 4 + z_lo), core: 2. Of those that a mesh axis runs over, the one named last changes fastest.
Arguments:
- q_proj: bfloat16 [8192, 8192], P('tensor', 'context'), may hold values from -6 to 6
- k_proj: bfloat16 [8192, 8192], P('tensor', 'context'), may hold values from -6 to 6
- v_proj: bfloat16 [8192, 8192], P('tensor', 'context'), may hold values from -6 to 6
- filter_taps: bfloat16 [512, 128], P('tensor'), may hold values from -0.5 to 0.5
- out_weight: bfloat16 [8192, 4096], P('tensor'), may hold values from -0.09375 to 0.09375
- cotangent: bfloat16 [8192, 4096], P('context', 'tensor'), may hold values from -6 to 6
Outputs:
- block_output: bfloat16 [8192, 4096], P('context', 'tensor')
- q_grad: bfloat16 [8192, 8192], P('tensor', 'context')
- k_grad: bfloat16 [8192, 8192], P('tensor', 'context')
- v_grad: bfloat16 [8192, 8192], P('tensor', 'context')
- filter_grad: float32 [512, 128], P('tensor')
The draws below stay inside these ranges and needn't reach their ends.
All inputs are finite; a program needn't handle non-finite values.
Results may differ from the reference program's by a relative error of at most 0.0064.
Values may be sent and summed in bfloat16 or wider, within the bound.
No kernel may reach another device: no remote copies, remote signals or barrier semaphores. Data moves between devices by JAX's collectives and lax.ppermute only.
A program may use at most 128 MiB of HBM per device.

```python
import math
import jax
import jax.numpy as jnp
from jax import lax

D = 8192
GROUPS = 512
DOUT = 4096
FL = 128
SEQ = 8192
GSIZE = 16


def with_spikes(drawn, own_key, source, target, parts, factor):
    def block_of(dim):
        return (jnp.arange(drawn.shape[dim]) // (drawn.shape[dim] // parts)).reshape((-1,) + (1,) * (drawn.ndim - 1 - dim))

    near = jax.random.permutation(own_key, parts)[block_of(target)]
    other_side = (block_of(target) + parts // 2) % parts
    return jnp.where((block_of(source) == near) | (block_of(source) == other_side), factor * drawn, drawn)


def levels(own_key, dims, pieces, smallest, largest):
    level = 1.0
    for position, blocks in pieces:
        draws = jax.random.uniform(jax.random.fold_in(jax.random.fold_in(own_key, 6), position), (blocks,), jnp.float32, smallest / len(pieces), largest / len(pieces))
        level = level * jnp.repeat(jnp.exp(draws), dims[position] // blocks).reshape((-1,) + (1,) * (len(dims) - 1 - position))
    return level


def centred(rng, shape, width, bound, pieces=(), held_as=jnp.bfloat16):
    result = jax.random.normal(rng, shape, jnp.float32) * width
    if len(pieces) > 0:
        result = levels(rng, shape, pieces, -0.22, 0.18) * result
    return jnp.clip(result, min=-bound, max=bound).astype(held_as)


def heavy_noise(own_key, shape, deviation, most, pieces, heavy, kind=jnp.bfloat16):
    array = deviation * jax.random.normal(own_key, shape, jnp.float32)
    if pieces:
        array = array * levels(own_key, shape, pieces, -0.22, 0.18)
    return jnp.clip(with_spikes(array, jax.random.fold_in(own_key, 3), *heavy), -most, most).astype(kind)


def setup_inputs(seed: int = 0) -> dict:
    key_list = jax.random.split(jax.random.key(seed), 7)
    q_proj = centred(key_list[0], (D, SEQ), 1.0, 6.0, ((0, 8), (1, 32)))
    k_proj = centred(key_list[1], (D, SEQ), 1.0, 6.0, ((0, 8), (1, 32)))
    v_proj = centred(key_list[2], (D, SEQ), 1.0, 6.0, ((0, 8), (1, 32)))
    filter_taps = centred(key_list[3], (GROUPS, FL), 0.09, 0.5, ((0, 8),))
    out_weight = heavy_noise(key_list[4], (D, DOUT), D ** -0.5, 0.09375, ((0, 8),), (0, 1, 8, 2.0))
    cotangent = centred(key_list[5], (SEQ, DOUT), 1.0, 6.0, ((0, 32), (1, 8)))
    return dict(q_proj=q_proj, k_proj=k_proj, v_proj=v_proj, filter_taps=filter_taps, out_weight=out_weight, cotangent=cotangent)


def toeplitz(taps_wide):
    index_rows = jnp.arange(FL)[:, None]
    index_cols = jnp.arange(2 * FL)[None, :]
    offsets = index_rows + FL - index_cols
    inside = (offsets >= 0) & (offsets < FL)
    picked = taps_wide[:, jnp.clip(offsets, 0, FL - 1).astype(jnp.int32)]
    return jnp.where(inside[None, :, :], picked, jnp.zeros_like(picked))

def causal_filter(signal, taps_wide):
    banded = toeplitz(taps_wide)
    blocks = signal.reshape(GROUPS, GSIZE, SEQ // FL, FL)
    earlier = jnp.concatenate([jnp.zeros_like(blocks[:, :, :1]), blocks[:, :, :-1]], axis=2)
    within = jnp.einsum('gij,gcbj->gcbi', banded[:, :, FL:], blocks, precision=lax.Precision.HIGHEST)
    before = jnp.einsum('gij,gcbj->gcbi', banded[:, :, :FL], earlier, precision=lax.Precision.HIGHEST)
    return (within + before).reshape(D, SEQ)

def reference(q_proj, k_proj, v_proj, filter_taps, out_weight, cotangent):
    q_wide = q_proj.astype(jnp.float32)
    k_wide = k_proj.astype(jnp.float32)
    v_wide = v_proj.astype(jnp.float32)
    product = (k_wide * v_wide).astype(jnp.bfloat16)
    product_wide = product.astype(jnp.float32)
    taps_wide = filter_taps.astype(jnp.float32)
    filter_out, pullback = jax.vjp(causal_filter, product_wide, taps_wide)
    filtered = filter_out.astype(jnp.bfloat16)
    filtered_wide = filtered.astype(jnp.float32)
    gated = (q_wide * filtered_wide).astype(jnp.bfloat16)
    block_output = jnp.dot(gated.T, out_weight, preferred_element_type=jnp.float32).astype(jnp.bfloat16)
    gated_grad = jnp.dot(out_weight, cotangent.T, preferred_element_type=jnp.float32)
    q_grad = (gated_grad * filtered_wide).astype(jnp.bfloat16)
    filtered_grad = (gated_grad * q_wide).astype(jnp.bfloat16)
    signal_grad, taps_grad = pullback(filtered_grad.astype(jnp.float32))
    product_grad = signal_grad.astype(jnp.bfloat16).astype(jnp.float32)
    k_grad = (product_grad * v_wide).astype(jnp.bfloat16)
    v_grad = (product_grad * k_wide).astype(jnp.bfloat16)
    filter_grad = taps_grad / math.sqrt(GSIZE * SEQ)
    return (block_output, q_grad, k_grad, v_grad, filter_grad)
```

```python
import math

import jax
import jax.numpy as jnp
from jax import lax
from jax.experimental import pallas as pl
from jax.experimental.pallas import tpu as pltpu
from jax.sharding import PartitionSpec as P

D = 8192
GROUPS = 512
FL = 128
GS = D // GROUPS
F32 = jnp.float32
BF = jnp.bfloat16
VM = pl.BlockSpec(memory_space=pltpu.VMEM)
SM = pl.BlockSpec(memory_space=pltpu.SMEM)
PARAMS = pltpu.CompilerParams(vmem_limit_bytes=24 << 20)


def call(kernel, outs, args, specs=None, scratch=(), name=None, flops=0, bytes_=0):
    return pl.pallas_call(
        kernel,
        out_shape=outs,
        in_specs=[VM] * len(args) if specs is None else specs,
        out_specs=jax.tree.map(lambda _: VM, outs),
        scratch_shapes=list(scratch),
        compiler_params=PARAMS,
        cost_estimate=pl.CostEstimate(flops=flops, bytes_accessed=bytes_, transcendentals=0),
        name=name,
    )(*args)


def shape(*dims, dt=BF):
    return jax.ShapeDtypeStruct(dims, dt)


def shear(row):
    return pltpu.roll(jnp.broadcast_to(row, (FL, 2 * FL)), 0, 1, stride=1, stride_axis=0)


def product_kernel(k_ref, v_ref, p0_ref, p1_ref):
    for half, ref in ((0, p0_ref), (1, p1_ref)):
        cols = slice(half * FL, (half + 1) * FL)
        ref[...] = (k_ref[:, cols].astype(F32) * v_ref[:, cols].astype(F32)).astype(BF)


def bands_kernel(taps_ref, fwd_ref, bwd_ref):
    taps = taps_ref[...].astype(F32)
    ahead = jnp.concatenate([taps, jnp.zeros_like(taps)], axis=1)
    row = lax.broadcasted_iota(jnp.int32, (FL, 2 * FL), 0)
    col = lax.broadcasted_iota(jnp.int32, (FL, 2 * FL), 1)
    mirror = ((row + col) % (2 * FL) == 0).astype(BF)
    back = jnp.dot(taps_ref[...], mirror, preferred_element_type=F32)
    for g in range(taps_ref.shape[0]):
        fwd = shear(ahead[g : g + 1]).astype(BF)
        bwd = shear(back[g : g + 1]).astype(BF)
        fwd_ref[g, :FL, :] = fwd[:, FL:]
        fwd_ref[g, FL:, :] = fwd[:, :FL]
        bwd_ref[g, :FL, :] = bwd[:, :FL]
        bwd_ref[g, FL:, :] = bwd[:, FL:]


def forward_kernel(half, place_ref, prev_ref, cur_ref, q_ref, band_ref, w_ref, fil_ref, mine_ref, other_ref, gated_t):
    cols = slice(half * FL, (half + 1) * FL)
    for g in range(band_ref.shape[0]):
        rows = slice(g * GS, (g + 1) * GS)
        window = jnp.concatenate([prev_ref[rows, :], cur_ref[rows, :]], axis=1)
        fil_ref[rows, :] = jnp.dot(window, band_ref[g], preferred_element_type=F32).astype(BF)
    gated = (q_ref[:, cols].astype(F32) * fil_ref[...].astype(F32)).astype(BF)
    gated_t[...] = gated.T
    z, core = place_ref[0], place_ref[1]
    width = mine_ref.shape[2]
    for k in range(mine_ref.shape[0]):
        for ref, side in ((mine_ref, core), (other_ref, 1 - core)):
            start = pl.multiple_of((2 * (z ^ k) + side) * width, width)
            ref[k] = jnp.dot(
                gated_t[...], w_ref[:, pl.ds(start, width)], preferred_element_type=F32
            ).astype(BF)


def gather_cot(place_ref, own_ref, own_other_ref, got_refs, got_other_ref, cot_t):
    z, core = place_ref[0], place_ref[1]
    width = own_ref.shape[1]
    for k in range(4):
        piece = own_ref[...] if k == 0 else got_refs[k - 1][...]
        other = own_other_ref[...] if k == 0 else got_other_ref[k - 1]
        for part, side in ((piece, core), (other, 1 - core)):
            start = pl.multiple_of((2 * (z ^ k) + side) * width, width)
            cot_t[pl.ds(start, width), :] = part.T


def grad_first_kernel(place_ref, own, own_other, g1, g2, g3, got_other, w_ref, q_ref, gg_ref, fg_ref, cot_t):
    gather_cot(place_ref, own, own_other, (g1, g2, g3), got_other, cot_t)
    gg = jnp.dot(w_ref[...], cot_t[...], preferred_element_type=F32)
    gg_ref[...] = gg
    fg_ref[...] = (gg * q_ref[:, :FL].astype(F32)).astype(BF)


def grad_second_kernel(
    place_ref, own, own_other, g1, g2, g3, got_other, w_ref, q_ref, gg0_ref, fg0_ref, fil0_ref, fil1_ref,
    halo_ref, p0_ref, p1_ref, qg_ref, fg_ref, taps_ref, cot_t, flip0, flip1,
):
    gather_cot(place_ref, own, own_other, (g1, g2, g3), got_other, cot_t)
    gg = jnp.dot(w_ref[...], cot_t[...], preferred_element_type=F32)
    fg = (gg * q_ref[:, FL:].astype(F32)).astype(BF)
    fg_ref[...] = fg
    qg_ref[:, FL:] = (gg * fil1_ref[...].astype(F32)).astype(BF)
    qg_ref[:, :FL] = (gg0_ref[...] * fil0_ref[...].astype(F32)).astype(BF)
    row = lax.broadcasted_iota(jnp.int32, (FL, FL), 0)
    col = lax.broadcasted_iota(jnp.int32, (FL, FL), 1)
    mirror = (row + col == FL - 1).astype(BF)
    flip0[...] = jnp.dot(fg0_ref[...], mirror, preferred_element_type=F32).astype(BF)
    flip1[...] = jnp.dot(fg_ref[...], mirror, preferred_element_type=F32).astype(BF)
    for g in range(taps_ref.shape[0]):
        rows = slice(g * GS, (g + 1) * GS)
        p0 = p0_ref[rows, :]
        grads = jnp.concatenate([flip0[rows, :], flip1[rows, :]], axis=0)
        window = jnp.concatenate(
            [
                jnp.concatenate([halo_ref[rows, :], p0], axis=1),
                jnp.concatenate([p0, p1_ref[rows, :]], axis=1),
            ],
            axis=0,
        )
        moments = lax.dot_general(
            grads, window, (((0,), (0,)), ((), ())), preferred_element_type=F32
        )
        sheared = pltpu.roll(moments, 0, 1, stride=1, stride_axis=0)
        taps_ref[g : g + 1, :] = jnp.sum(sheared[:, FL:], axis=0, keepdims=True)


def backward_kernel(fg0_ref, fg1_ref, next_ref, band_ref, k_ref, v_ref, kg_ref, vg_ref):
    for g in range(band_ref.shape[0]):
        rows = slice(g * GS, (g + 1) * GS)
        fg1 = fg1_ref[rows, :]
        window = jnp.concatenate(
            [
                jnp.concatenate([fg0_ref[rows, :], fg1], axis=1),
                jnp.concatenate([fg1, next_ref[rows, :]], axis=1),
            ],
            axis=0,
        )
        both = jnp.dot(window, band_ref[g], preferred_element_type=F32).astype(BF).astype(F32)
        pg = jnp.concatenate([both[:GS], both[GS:]], axis=1)
        kg_ref[rows, :] = (pg * v_ref[rows, :].astype(F32)).astype(BF)
        vg_ref[rows, :] = (pg * k_ref[rows, :].astype(F32)).astype(BF)


def body(q_proj, k_proj, v_proj, filter_taps, out_weight, cotangent):
    chans, toks = q_proj.shape
    groups = filter_taps.shape[0]
    feats = out_weight.shape[1]
    width = cotangent.shape[1]
    n_ctx, n_ten = lax.axis_size("context"), lax.axis_size("tensor")
    scale = 1.0 / math.sqrt(GS * toks * n_ctx)
    zs = n_ten // 2
    me = lax.axis_index("tensor")
    place = jnp.stack([me // 2, me % 2]).astype(jnp.int32)

    def across(array, k):
        return lax.ppermute(array, "tensor", [(j, j ^ k) for j in range(n_ten)])

    p0, p1 = call(product_kernel, [shape(chans, FL)] * 2, (k_proj, v_proj), name="product")
    halo = lax.ppermute(p1, "context", [(i, i + 1) for i in range(n_ctx - 1)])

    cots = []
    for half in range(2):
        own = cotangent[half * FL : (half + 1) * FL]
        own_other = across(own, 1)
        got = [across(own, 2 * k) for k in range(1, zs)]
        got_other = across(jnp.stack(got), 1)
        cots.append((own, own_other, *got, got_other))

    band_f, band_b = call(bands_kernel, [shape(groups, 2 * FL, FL)] * 2, (filter_taps,), name="bands")

    def forward(half, prev, cur):
        fil, mine, other = call(
            lambda *refs: forward_kernel(half, *refs),
            [shape(chans, FL), shape(zs, FL, width), shape(zs, FL, width)],
            (place, prev, cur, q_proj, band_f, out_weight),
            specs=[SM] + [VM] * 5,
            scratch=[pltpu.VMEM((FL, chans), BF)],
            name=f"forward{half}",
            flops=2 * chans * FL * feats,
        )
        swapped = across(other, 1)
        total = mine.astype(F32) + swapped.astype(F32)
        rest = [across(total[k].astype(BF), 2 * k) for k in range(1, zs)]
        return fil, (total[0], rest)

    def finish(total, rest):
        for r in rest:
            total = total + r.astype(F32)
        return total.astype(BF)

    fil1, out1 = forward(1, p0, p1)

    n_cot = len(cots[0])
    gg0, fg0 = call(
        grad_first_kernel,
        [shape(chans, FL, dt=F32), shape(chans, FL)],
        (place, *cots[0], out_weight, q_proj),
        specs=[SM] + [VM] * (n_cot + 2),
        scratch=[pltpu.VMEM((feats, FL), BF)],
        name="grad0",
        flops=2 * chans * FL * feats,
    )
    after = lax.ppermute(fg0, "context", [(i + 1, i) for i in range(n_ctx - 1)])

    fil0, out0 = forward(0, halo, p0)

    q_grad, fg1, taps_part = call(
        grad_second_kernel,
        [shape(chans, toks), shape(chans, FL), shape(groups, FL, dt=F32)],
        (place, *cots[1], out_weight, q_proj, gg0, fg0, fil0, fil1, halo, p0, p1),
        specs=[SM] + [VM] * (n_cot + 9),
        scratch=[pltpu.VMEM((feats, FL), BF), pltpu.VMEM((chans, FL), BF), pltpu.VMEM((chans, FL), BF)],
        name="grad1",
        flops=2 * chans * FL * feats,
    )
    step = 1
    while step < n_ctx:
        taps_part = taps_part + lax.ppermute(
            taps_part, "context", [(i, i ^ step) for i in range(n_ctx)]
        )
        step *= 2
    filter_grad = taps_part[:, ::-1] * scale

    k_grad, v_grad = call(
        backward_kernel,
        [shape(chans, toks)] * 2,
        (fg0, fg1, after, band_b, k_proj, v_proj),
        name="backward",
    )
    block_output = jnp.concatenate([finish(*out0), finish(*out1)], axis=0)
    return (block_output, q_grad, k_grad, v_grad, filter_grad)


def solution(mesh):
    placed = (
        P("tensor", "context"),
        P("tensor", "context"),
        P("tensor", "context"),
        P("tensor", None),
        P("tensor", None),
        P("context", "tensor"),
    )
    return jax.shard_map(
        body,
        mesh=mesh,
        in_specs=placed,
        out_specs=(
            P("context", "tensor"),
            P("tensor", "context"),
            P("tensor", "context"),
            P("tensor", "context"),
            P("tensor", None),
        ),
        check_vma=False,
    )
```

```python
import math

import jax
import jax.numpy as jnp
from jax import lax
from jax.experimental import pallas as pl
from jax.experimental.pallas import tpu as pltpu
from jax.sharding import PartitionSpec as P

D = 8192
GROUPS = 512
FL = 128
GS = D // GROUPS
F32 = jnp.float32
BF = jnp.bfloat16
VM = pl.BlockSpec(memory_space=pltpu.VMEM)
SM = pl.BlockSpec(memory_space=pltpu.SMEM)
PARAMS = pltpu.CompilerParams(vmem_limit_bytes=16 << 20)


def call(kernel, outs, args, specs=None, out_specs=None, scratch=(), name=None):
    return pl.pallas_call(
        kernel,
        out_shape=outs,
        in_specs=[VM] * len(args) if specs is None else specs,
        out_specs=[VM] * len(outs) if out_specs is None else out_specs,
        scratch_shapes=list(scratch),
        compiler_params=PARAMS,
        cost_estimate=pl.CostEstimate(flops=1, bytes_accessed=1, transcendentals=0),
        name=name,
    )(*args)


def shape(*dims, dt=BF):
    return jax.ShapeDtypeStruct(dims, dt)


def shear(row):
    return pltpu.roll(jnp.broadcast_to(row, (FL, 2 * FL)), 0, 1, stride=1, stride_axis=0)


def flip(array):
    row = lax.broadcasted_iota(jnp.int32, (FL, FL), 0)
    col = lax.broadcasted_iota(jnp.int32, (FL, FL), 1)
    return jnp.dot(array, (row + col == FL - 1).astype(BF), preferred_element_type=F32).astype(BF)


def half_cols(half):
    return slice(half * FL, (half + 1) * FL)


def filter_kernel(prev_ref, cur_ref, band, fil_ref, *flips):
    for ref, flipped in zip((prev_ref, cur_ref), flips):
        flipped[...] = flip(ref[...])
    for g in range(band.shape[0]):
        rows = slice(g * GS, (g + 1) * GS)
        window = jnp.concatenate([prev_ref[rows, :], cur_ref[rows, :]], axis=1)
        fil_ref[rows, :] = jnp.dot(window, band[g], preferred_element_type=F32).astype(BF)


def project_kernel(place_ref, prev_ref, cur_ref, q_ref, fil1_ref, band, w_ref, fil0_ref, mine_ref, other_ref, flip_ref, gated_t):
    filter_kernel(prev_ref, cur_ref, band, fil0_ref, flip_ref)
    for half, fil_ref in enumerate((fil0_ref, fil1_ref)):
        cols = half_cols(half)
        gated_t[cols, :] = (q_ref[:, cols].astype(F32) * fil_ref[...].astype(F32)).astype(BF).T
    z, core = place_ref[0], place_ref[1]
    chips, _, width = mine_ref.shape
    for k in range(chips):
        for ref, side in ((other_ref, 1 - core), (mine_ref, core)):
            start = pl.multiple_of((2 * (z ^ k) + side) * width, width)
            ref[k] = jnp.dot(
                gated_t[...], w_ref[:, pl.ds(start, width)], preferred_element_type=F32
            ).astype(BF)


def bands_kernel(taps_ref, fwd_ref, bwd_ref):
    taps = taps_ref[...].astype(F32)
    ahead = jnp.concatenate([taps, jnp.zeros_like(taps)], axis=1)
    row = lax.broadcasted_iota(jnp.int32, (FL, 2 * FL), 0)
    col = lax.broadcasted_iota(jnp.int32, (FL, 2 * FL), 1)
    wrap = ((row + col) % (2 * FL) == 0).astype(BF)
    back = jnp.dot(taps_ref[...], wrap, preferred_element_type=F32)
    for g in range(taps_ref.shape[0]):
        fwd = shear(ahead[g : g + 1]).astype(BF)
        bwd = shear(back[g : g + 1]).astype(BF)
        fwd_ref[g, :FL, :] = fwd[:, FL:]
        fwd_ref[g, FL:, :] = fwd[:, :FL]
        bwd_ref[g, :FL, :] = bwd[:, :FL]
        bwd_ref[g, FL:, :] = bwd[:, FL:]


def grad_kernel(place_ref, own_ref, g1, g2, g3, mate_ref, w_ref, q_ref, gg_ref, fg0_ref, fg1_ref, cot_t):
    z, core = place_ref[0], place_ref[1]
    width = own_ref.shape[1]
    for k, got in enumerate((own_ref, g1, g2, g3)):
        for piece, side in ((got[...], core), (mate_ref[k], 1 - core)):
            start = pl.multiple_of((2 * (z ^ k) + side) * width, width)
            cot_t[pl.ds(start, width), :] = piece.T
    gg_ref[...] = jnp.dot(w_ref[...], cot_t[...], preferred_element_type=F32)
    for half, fg_ref in enumerate((fg0_ref, fg1_ref)):
        cols = half_cols(half)
        fg_ref[...] = (gg_ref[:, cols] * q_ref[:, cols].astype(F32)).astype(BF)


def taps_kernel(scale, fg0_ref, fg_ref, fliph, flip0, flip1, taps_ref):
    for g in range(taps_ref.shape[0]):
        rows = slice(g * GS, (g + 1) * GS)
        mid = flip0[rows, :]
        grads = jnp.concatenate([fg0_ref[rows, :], fg_ref[rows, :]], axis=0)
        window = jnp.concatenate(
            [
                jnp.concatenate([mid, fliph[rows, :]], axis=1),
                jnp.concatenate([flip1[rows, :], mid], axis=1),
            ],
            axis=0,
        )
        moments = lax.dot_general(
            grads, window, (((0,), (0,)), ((), ())), preferred_element_type=F32
        )
        sheared = pltpu.roll(moments, 1, 1, stride=1, stride_axis=0)
        taps_ref[g : g + 1, :] = jnp.sum(sheared[:, FL:], axis=0, keepdims=True) * scale


def backward_kernel(
    fg0_ref, fg1_ref, next_ref, band_ref, k_ref, v_ref, gg_ref, fil0_ref, fil1_ref, kg_ref, vg_ref, qg_ref
):
    qg_ref[:, :FL] = (gg_ref[:, :FL] * fil0_ref[...].astype(F32)).astype(BF)
    qg_ref[:, FL:] = (gg_ref[:, FL:] * fil1_ref[...].astype(F32)).astype(BF)
    for g in range(band_ref.shape[0]):
        rows = slice(g * GS, (g + 1) * GS)
        fg1 = fg1_ref[rows, :]
        window = jnp.concatenate(
            [
                jnp.concatenate([fg0_ref[rows, :], fg1], axis=1),
                jnp.concatenate([fg1, next_ref[rows, :]], axis=1),
            ],
            axis=0,
        )
        both = jnp.dot(window, band_ref[g], preferred_element_type=F32).astype(BF).astype(F32)
        pg = jnp.concatenate([both[:GS], both[GS:]], axis=1)
        kg_ref[rows, :] = (pg * v_ref[rows, :].astype(F32)).astype(BF)
        vg_ref[rows, :] = (pg * k_ref[rows, :].astype(F32)).astype(BF)


def wave(*values):
    return lax.optimization_barrier(values)


def shift_pairs(n_ctx, n_ten, by):
    ys, halves = 4, 2
    zs = n_ten // 2
    at = lambda x, z, y, core: ((x * halves + z // zs) * ys + y) * n_ten + (z % zs) * 2 + core
    direct, first, second = [], [], []
    for i in range(n_ctx):
        j = i + by
        if not 0 <= j < n_ctx:
            continue
        for t in range(n_ten):
            source, target = i * n_ten + t, j * n_ten + t
            direct.append((source, target))
            if i // ys == j // ys:
                first.append((source, target))
            else:
                z, z_half = (i // ys % halves) * zs + t // 2, zs // 2
                relay = at(i // (ys * halves), (z - z_half) % (halves * zs), j % ys, t % 2)
                first.append((source, relay))
                second.append((relay, target))
    return direct, first, second


def body(q_proj, k_proj, v_proj, filter_taps, out_weight, cotangent):
    chans, toks = q_proj.shape
    groups = filter_taps.shape[0]
    feats = out_weight.shape[1]
    width = cotangent.shape[1]
    n_ctx, n_ten = lax.axis_size("context"), lax.axis_size("tensor")
    scale = 1.0 / math.sqrt(GS * toks * n_ctx)
    zs = n_ten // 2
    me = lax.axis_index("tensor")
    place = jnp.stack([me // 2, me % 2]).astype(jnp.int32)
    half_shape = shape(chans, FL)
    gg_shape = shape(chans, toks, dt=F32)

    def move(name, array, axis, pairs):
        with jax.named_scope(name):
            return lax.ppermute(array, axis, pairs)

    def swap(name, array):
        return move(name, array, "tensor", [(j, j ^ 1) for j in range(n_ten)])

    def shift_first(name, array, by):
        direct, first, _ = shift_pairs(n_ctx, n_ten, by)
        cut = chans * 3 // 8
        axes = ("context", "tensor")
        return move(f"{name}_direct", array[:cut], axes, direct), move(f"{name}_relay", array[cut:], axes, first)

    def shift_second(name, relayed, by):
        _, _, second = shift_pairs(n_ctx, n_ten, by)
        return move(f"{name}_end", relayed, ("context", "tensor"), second)

    def shift_join(direct, relayed, end, by):
        ys = 4
        at_end = lax.axis_index("context") % ys == (0 if by > 0 else ys - 1)
        return jnp.concatenate([direct, jnp.where(at_end, end, relayed)], axis=0)

    def exchange(name, array, k):
        return move(f"{name}{k}", array, "tensor", [(j, j ^ (2 * k)) for j in range(n_ten)])

    def taps_phase(part, steps):
        got = [move(f"taps_{s}", part, "context", [(i, i ^ s) for i in range(n_ctx)]) for s in steps]
        if len(got) == 1:
            return part + got[0]
        return (part + got[0]) + (got[1] + got[2])

    got = [exchange("cot", cotangent, k) for k in range(1, zs)]
    p1, p0 = [
        (k_proj[:, c].astype(F32) * v_proj[:, c].astype(F32)).astype(BF) for c in map(half_cols, (1, 0))
    ]
    band_f, band_b = call(bands_kernel, [shape(groups, 2 * FL, FL)] * 2, (filter_taps,), name="bands")
    fil1, flip0, flip1 = call(filter_kernel, [half_shape] * 3, (p0, p1, band_f), name="filter1")
    halo = move("halo", p1, "context", [(i, i + 1) for i in range(n_ctx - 1)])
    fil0, mine, other, fliph = call(
        project_kernel,
        [half_shape, shape(zs, toks, width), shape(zs, toks, width), half_shape],
        (place, halo, p0, q_proj, fil1, band_f, out_weight),
        specs=[SM] + [VM] * 6,
        scratch=[pltpu.VMEM((toks, chans), BF)],
        name="project",
    )
    there = swap("out_swap", other)

    *got, fil0 = wave(*got, fil0)
    mate = swap("cot_swap", jnp.stack([cotangent, *got]))
    gg, fg0, fg1 = call(
        grad_kernel,
        [gg_shape, half_shape, half_shape],
        (place, cotangent, *got, mate, out_weight, q_proj),
        specs=[SM] + [VM] * (zs + 3),
        scratch=[pltpu.VMEM((feats, toks), BF)],
        name="grad",
    )
    after = move("after", fg0, "context", [(i + 1, i) for i in range(n_ctx - 1)])

    (taps_part,) = call(
        lambda *refs: taps_kernel(scale, *refs),
        [shape(groups, FL, dt=F32)],
        (fg0, fg1, fliph, flip0, flip1),
        name="taps",
    )
    there, taps_done = wave(there, taps_part)
    total = mine.astype(F32) + there.astype(F32)
    rest = [exchange("out", total[k].astype(BF), k) for k in range(1, zs)]
    for s in (8, 16, 1):
        taps_part = taps_phase(taps_part, [s])
    after, taps_part = wave(after, taps_part)
    k_grad, v_grad, q_grad = call(
        backward_kernel,
        [shape(chans, toks)] * 3,
        (fg0, fg1, after, band_b, k_proj, v_proj, gg, fil0, fil1),
        name="backward",
    )
    for s in (2, 4):
        taps_part = taps_phase(taps_part, [s])
    block_output = total[0]
    for r in rest:
        block_output = block_output + r.astype(F32)
    return (block_output.astype(BF), q_grad, k_grad, v_grad, taps_part)


def solution(mesh):
    placed = (
        P("tensor", "context"),
        P("tensor", "context"),
        P("tensor", "context"),
        P("tensor", None),
        P("tensor", None),
        P("context", "tensor"),
    )
    return jax.shard_map(
        body,
        mesh=mesh,
        in_specs=placed,
        out_specs=(
            P("context", "tensor"),
            P("tensor", "context"),
            P("tensor", "context"),
            P("tensor", "context"),
            P("tensor", None),
        ),
        check_vma=False,
    )
```

```python
import math

import jax
import jax.numpy as jnp
from jax import lax
from jax.experimental import pallas as pl
from jax.experimental.pallas import tpu as pltpu
from jax.sharding import PartitionSpec as P

D = 8192
GROUPS = 512
FL = 128
GS = D // GROUPS
F32 = jnp.float32
BF = jnp.bfloat16
VM = pl.BlockSpec(memory_space=pltpu.VMEM)
SM = pl.BlockSpec(memory_space=pltpu.SMEM)
PARAMS = pltpu.CompilerParams(vmem_limit_bytes=16 << 20)


def call(kernel, outs, args, specs=None, out_specs=None, scratch=(), name=None):
    return pl.pallas_call(
        kernel,
        out_shape=outs,
        in_specs=[VM] * len(args) if specs is None else specs,
        out_specs=[VM] * len(outs) if out_specs is None else out_specs,
        scratch_shapes=list(scratch),
        compiler_params=PARAMS,
        cost_estimate=pl.CostEstimate(flops=1, bytes_accessed=1, transcendentals=0),
        name=name,
    )(*args)


def shape(*dims, dt=BF):
    return jax.ShapeDtypeStruct(dims, dt)


def shear(row):
    return pltpu.roll(jnp.broadcast_to(row, (FL, 2 * FL)), 0, 1, stride=1, stride_axis=0)


def flip(array):
    row = lax.broadcasted_iota(jnp.int32, (FL, FL), 0)
    col = lax.broadcasted_iota(jnp.int32, (FL, FL), 1)
    return jnp.dot(array, (row + col == FL - 1).astype(BF), preferred_element_type=F32).astype(BF)


def half_cols(half):
    return slice(half * FL, (half + 1) * FL)


def forward_bands(taps_ref, band):
    taps = taps_ref[...].astype(F32)
    ahead = jnp.concatenate([taps, jnp.zeros_like(taps)], axis=1)
    for g in range(taps.shape[0]):
        fwd = shear(ahead[g : g + 1]).astype(BF)
        band[g, :FL, :] = fwd[:, FL:]
        band[g, FL:, :] = fwd[:, :FL]


def run_filter(prev_ref, cur_ref, band, fil_ref):
    for g in range(band.shape[0]):
        rows = slice(g * GS, (g + 1) * GS)
        window = jnp.concatenate([prev_ref[rows, :], cur_ref[rows, :]], axis=1)
        fil_ref[rows, :] = jnp.dot(window, band[g], preferred_element_type=F32).astype(BF)


def filter_kernel(place_ref, p0_ref, p1_ref, taps_ref, q_ref, w_ref, fil_ref, mine_ref, other_ref, flip0_ref, flip1_ref, gated_t, band):
    forward_bands(taps_ref, band)
    flip0_ref[...] = flip(p0_ref[...])
    flip1_ref[...] = flip(p1_ref[...])
    run_filter(p0_ref, p1_ref, band, fil_ref)
    project(1, place_ref, q_ref, fil_ref, w_ref, mine_ref, other_ref, gated_t)


def project(half, place_ref, q_ref, fil_ref, w_ref, mine_ref, other_ref, gated_t):
    gated_t[...] = (q_ref[:, half_cols(half)].astype(F32) * fil_ref[...].astype(F32)).astype(BF).T
    z, core = place_ref[0], place_ref[1]
    chips, _, width = mine_ref.shape
    for k in range(chips):
        for ref, side in ((other_ref, 1 - core), (mine_ref, core)):
            start = pl.multiple_of((2 * (z ^ k) + side) * width, width)
            ref[k] = jnp.dot(
                gated_t[...], w_ref[:, pl.ds(start, width)], preferred_element_type=F32
            ).astype(BF)


def filter_first_kernel(
    place_ref, near_ref, far_ref, direct_ref, p0_ref, taps_ref, q_ref, w_ref,
    fil_ref, mine_ref, other_ref, flip_ref, gated_t, band, halo,
):
    cut = near_ref.shape[0]
    halo[:cut, :] = jnp.where(place_ref[2] == 1, far_ref[...], near_ref[...])
    halo[cut:, :] = direct_ref[...]
    forward_bands(taps_ref, band)
    flip_ref[...] = flip(halo[...])
    run_filter(halo, p0_ref, band, fil_ref)
    project(0, place_ref, q_ref, fil_ref, w_ref, mine_ref, other_ref, gated_t)


def grad_kernel(place_ref, own_ref, g1, g2, g3, mate_ref, w_ref, q_ref, gg_ref, fg0_ref, fg1_ref, cot_t):
    z, core = place_ref[0], place_ref[1]
    width = own_ref.shape[1]
    for k, got in enumerate((own_ref, g1, g2, g3)):
        for piece, side in ((got[...], core), (mate_ref[k], 1 - core)):
            start = pl.multiple_of((2 * (z ^ k) + side) * width, width)
            cot_t[pl.ds(start, width), :] = piece.T
    gg_ref[...] = jnp.dot(w_ref[...], cot_t[...], preferred_element_type=F32)
    for half, fg_ref in enumerate((fg0_ref, fg1_ref)):
        cols = half_cols(half)
        fg_ref[...] = (gg_ref[:, cols] * q_ref[:, cols].astype(F32)).astype(BF)


def taps_kernel(scale, fg0_ref, fg_ref, fliph, flip0, flip1, taps_ref):
    for g in range(taps_ref.shape[0]):
        rows = slice(g * GS, (g + 1) * GS)
        mid = flip0[rows, :]
        grads = jnp.concatenate([fg0_ref[rows, :], fg_ref[rows, :]], axis=0)
        window = jnp.concatenate(
            [
                jnp.concatenate([mid, fliph[rows, :]], axis=1),
                jnp.concatenate([flip1[rows, :], mid], axis=1),
            ],
            axis=0,
        )
        moments = lax.dot_general(
            grads, window, (((0,), (0,)), ((), ())), preferred_element_type=F32
        )
        sheared = pltpu.roll(moments, 1, 1, stride=1, stride_axis=0)
        taps_ref[g : g + 1, :] = jnp.sum(sheared[:, FL:], axis=0, keepdims=True) * scale


def backward_kernel(
    fg0_ref, fg1_ref, next_ref, taps_ref, k_ref, v_ref, gg_ref, fil0_ref, fil1_ref, kg_ref, vg_ref, qg_ref
):
    row = lax.broadcasted_iota(jnp.int32, (FL, 2 * FL), 0)
    col = lax.broadcasted_iota(jnp.int32, (FL, 2 * FL), 1)
    wrap = ((row + col) % (2 * FL) == 0).astype(BF)
    back = jnp.dot(taps_ref[...], wrap, preferred_element_type=F32)
    qg_ref[:, :FL] = (gg_ref[:, :FL] * fil0_ref[...].astype(F32)).astype(BF)
    qg_ref[:, FL:] = (gg_ref[:, FL:] * fil1_ref[...].astype(F32)).astype(BF)
    for g in range(taps_ref.shape[0]):
        rows = slice(g * GS, (g + 1) * GS)
        bwd = shear(back[g : g + 1]).astype(BF)
        band = jnp.concatenate([bwd[:, :FL], bwd[:, FL:]], axis=0)
        fg1 = fg1_ref[rows, :]
        window = jnp.concatenate(
            [
                jnp.concatenate([fg0_ref[rows, :], fg1], axis=1),
                jnp.concatenate([fg1, next_ref[rows, :]], axis=1),
            ],
            axis=0,
        )
        both = jnp.dot(window, band, preferred_element_type=F32).astype(BF).astype(F32)
        pg = jnp.concatenate([both[:GS], both[GS:]], axis=1)
        kg_ref[rows, :] = (pg * v_ref[rows, :].astype(F32)).astype(BF)
        vg_ref[rows, :] = (pg * k_ref[rows, :].astype(F32)).astype(BF)


def wave(*values):
    return lax.optimization_barrier(values)


def shift_pairs(n_ctx, n_ten, by):
    ys, halves = 4, 2
    zs = n_ten // 2
    at = lambda x, z, y, core: ((x * halves + z // zs) * ys + y) * n_ten + (z % zs) * 2 + core
    direct, first, second = [], [], []
    for i in range(n_ctx):
        j = i + by
        if not 0 <= j < n_ctx:
            continue
        for t in range(n_ten):
            source, target = i * n_ten + t, j * n_ten + t
            direct.append((source, target))
            if i // ys == j // ys:
                first.append((source, target))
            else:
                relay = at(i // (ys * halves), (i // ys % halves) * zs + t // 2, j % ys, t % 2)
                first.append((source, relay))
                second.append((relay, target))
    return direct, first, second


def body(q_proj, k_proj, v_proj, filter_taps, out_weight, cotangent):
    chans, toks = q_proj.shape
    groups = filter_taps.shape[0]
    feats = out_weight.shape[1]
    width = cotangent.shape[1]
    n_ctx, n_ten = lax.axis_size("context"), lax.axis_size("tensor")
    scale = 1.0 / math.sqrt(GS * toks * n_ctx)
    zs = n_ten // 2
    me = lax.axis_index("tensor")
    place = jnp.stack([me // 2, me % 2, (lax.axis_index("context") % 4 == 0)]).astype(jnp.int32)
    half_shape = shape(chans, FL)
    gg_shape = shape(chans, toks, dt=F32)

    def move(name, array, axis, pairs):
        with jax.named_scope(name):
            return lax.ppermute(array, axis, pairs)

    def swap(name, array):
        return move(name, array, "tensor", [(j, j ^ 1) for j in range(n_ten)])

    def exchange(name, array, k):
        return move(f"{name}{k}", array, "tensor", [(j, j ^ (2 * k)) for j in range(n_ten)])

    def taps_phase(part, steps):
        got = [move(f"taps_{s}", part, "context", [(i, i ^ s) for i in range(n_ctx)]) for s in steps]
        if len(got) == 1:
            return part + got[0]
        return (part + got[0]) + (got[1] + got[2])

    got = [exchange("cot", cotangent, k) for k in range(1, zs)]
    p1, p0 = [
        (k_proj[:, c].astype(F32) * v_proj[:, c].astype(F32)).astype(BF) for c in map(half_cols, (1, 0))
    ]
    axes = ("context", "tensor")
    direct_pairs, first, second = shift_pairs(n_ctx, n_ten, 1)
    cut = chans // 2
    near = move("halo_near", p1[:cut], axes, first)
    out_half = shape(zs, FL, width)
    scratch = [pltpu.VMEM((FL, chans), BF), pltpu.VMEM((groups, 2 * FL, FL), BF)]
    fil1, mine1, other1, flip0, flip1 = call(
        filter_kernel,
        [half_shape, out_half, out_half, half_shape, half_shape],
        (place, p0, p1, filter_taps, q_proj, out_weight),
        specs=[SM] + [VM] * 5,
        scratch=scratch,
        name="forward1",
    )
    direct = move("halo_direct", p1[cut:], axes, direct_pairs)
    far = move("halo_far", near, axes, second)
    *got, direct, far, other1 = wave(*got, direct, far, other1)

    mate = swap("cot_swap", jnp.stack([cotangent, *got]))
    there1 = swap("out1_swap", other1)
    fil0, mine0, other0, fliph = call(
        filter_first_kernel,
        [half_shape, out_half, out_half, half_shape],
        (place, near, far, direct, p0, filter_taps, q_proj, out_weight),
        specs=[SM] + [VM] * 7,
        scratch=scratch + [pltpu.VMEM((chans, FL), BF)],
        name="forward0",
    )
    there0 = swap("out0_swap", other0)
    mate, fil0 = wave(mate, fil0)
    gg, fg0, fg1 = call(
        grad_kernel,
        [gg_shape, half_shape, half_shape],
        (place, cotangent, *got, mate, out_weight, q_proj),
        specs=[SM] + [VM] * (zs + 3),
        scratch=[pltpu.VMEM((feats, toks), BF)],
        name="grad",
    )
    after = move("after", fg0, "context", [(i + 1, i) for i in range(n_ctx - 1)])
    near, fg1 = wave(near, fg1)
    (taps_part,) = call(
        lambda *refs: taps_kernel(scale, *refs),
        [shape(groups, FL, dt=F32)],
        (fg0, fg1, fliph, flip0, flip1),
        name="taps",
    )
    total = jnp.concatenate(
        [m.astype(F32) + t.astype(F32) for m, t in ((mine0, there0), (mine1, there1))], axis=1
    )
    rest = [exchange("out", total[k].astype(BF), k) for k in range(1, zs)]
    taps_part = taps_phase(taps_part, [8])
    taps_part = taps_phase(taps_part, [16])
    taps_part = taps_phase(taps_part, [1])
    after, taps_part = wave(after, taps_part)
    k_grad, v_grad, q_grad = call(
        backward_kernel,
        [shape(chans, toks)] * 3,
        (fg0, fg1, after, filter_taps, k_proj, v_proj, gg, fil0, fil1),
        name="backward",
    )
    taps_part = taps_phase(taps_part, [2])
    taps_part, k_grad = wave(taps_part, k_grad)
    taps_part = taps_phase(taps_part, [4])
    block_output = total[0]
    for part in rest:
        block_output = block_output + part.astype(F32)
    block_output = block_output.astype(BF)
    return (block_output, q_grad, k_grad, v_grad, taps_part)


def solution(mesh):
    placed = (
        P("tensor", "context"),
        P("tensor", "context"),
        P("tensor", "context"),
        P("tensor", None),
        P("tensor", None),
        P("context", "tensor"),
    )
    return jax.shard_map(
        body,
        mesh=mesh,
        in_specs=placed,
        out_specs=(
            P("context", "tensor"),
            P("tensor", "context"),
            P("tensor", "context"),
            P("tensor", "context"),
            P("tensor", None),
        ),
        check_vma=False,
    )
```

```python
import math

import jax
import jax.numpy as jnp
from jax import lax
from jax.experimental import pallas as pl
from jax.experimental.pallas import tpu as pltpu
from jax.sharding import PartitionSpec as P

D = 8192
GROUPS = 512
FL = 128
GS = D // GROUPS
F32 = jnp.float32
BF = jnp.bfloat16
VM = pl.BlockSpec(memory_space=pltpu.VMEM)
SM = pl.BlockSpec(memory_space=pltpu.SMEM)
PARAMS = pltpu.CompilerParams(vmem_limit_bytes=16 << 20)


def call(kernel, outs, args, specs=None, out_specs=None, scratch=(), name=None):
    return pl.pallas_call(
        kernel,
        out_shape=outs,
        in_specs=[VM] * len(args) if specs is None else specs,
        out_specs=[VM] * len(outs) if out_specs is None else out_specs,
        scratch_shapes=list(scratch),
        compiler_params=PARAMS,
        cost_estimate=pl.CostEstimate(flops=1, bytes_accessed=1, transcendentals=0),
        name=name,
    )(*args)


def shape(*dims, dt=BF):
    return jax.ShapeDtypeStruct(dims, dt)


def shear(row):
    return pltpu.roll(jnp.broadcast_to(row, (FL, 2 * FL)), 0, 1, stride=1, stride_axis=0)


def flip(array):
    row = lax.broadcasted_iota(jnp.int32, (FL, FL), 0)
    col = lax.broadcasted_iota(jnp.int32, (FL, FL), 1)
    return jnp.dot(array, (row + col == FL - 1).astype(BF), preferred_element_type=F32).astype(BF)


def half_cols(half):
    return slice(half * FL, (half + 1) * FL)


def forward_bands(taps_ref, band):
    taps = taps_ref[...].astype(F32)
    ahead = jnp.concatenate([taps, jnp.zeros_like(taps)], axis=1)
    for g in range(taps.shape[0]):
        fwd = shear(ahead[g : g + 1]).astype(BF)
        band[g, :FL, :] = fwd[:, FL:]
        band[g, FL:, :] = fwd[:, :FL]


def run_filter(prev_ref, cur_ref, band, fil_ref):
    for g in range(band.shape[0]):
        rows = slice(g * GS, (g + 1) * GS)
        window = jnp.concatenate([prev_ref[rows, :], cur_ref[rows, :]], axis=1)
        fil_ref[rows, :] = jnp.dot(window, band[g], preferred_element_type=F32).astype(BF)


def filter_kernel(place_ref, p0_ref, p1_ref, taps_ref, q_ref, w_ref, fil_ref, mine_ref, other_ref, flip0_ref, flip1_ref, gated_t, band):
    forward_bands(taps_ref, band)
    flip0_ref[...] = flip(p0_ref[...])
    flip1_ref[...] = flip(p1_ref[...])
    run_filter(p0_ref, p1_ref, band, fil_ref)
    project(1, place_ref, q_ref, fil_ref, w_ref, mine_ref, other_ref, gated_t)


def project(half, place_ref, q_ref, fil_ref, w_ref, mine_ref, other_ref, gated_t):
    gated_t[...] = (q_ref[:, half_cols(half)].astype(F32) * fil_ref[...].astype(F32)).astype(BF).T
    z, core = place_ref[0], place_ref[1]
    chips, _, width = mine_ref.shape
    for k in range(chips):
        for ref, side in ((other_ref, 1 - core), (mine_ref, core)):
            start = pl.multiple_of((2 * (z ^ k) + side) * width, width)
            ref[k] = jnp.dot(
                gated_t[...], w_ref[:, pl.ds(start, width)], preferred_element_type=F32
            ).astype(BF)


def filter_first_kernel(
    place_ref, near_ref, far_ref, direct_ref, p0_ref, taps_ref, q_ref, w_ref,
    fil_ref, mine_ref, other_ref, flip_ref, gated_t, band, halo,
):
    cut = near_ref.shape[0]
    halo[:cut, :] = jnp.where(place_ref[2] == 1, far_ref[...], near_ref[...])
    halo[cut:, :] = direct_ref[...]
    forward_bands(taps_ref, band)
    flip_ref[...] = flip(halo[...])
    run_filter(halo, p0_ref, band, fil_ref)
    project(0, place_ref, q_ref, fil_ref, w_ref, mine_ref, other_ref, gated_t)


def grad_kernel(place_ref, own_ref, g1, g2, g3, mate_ref, w_ref, q_ref, gg_ref, fg0_ref, fg1_ref, cot_t):
    z, core = place_ref[0], place_ref[1]
    width = own_ref.shape[1]
    for k, got in enumerate((own_ref, g1, g2, g3)):
        for piece, side in ((got[...], core), (mate_ref[k], 1 - core)):
            start = pl.multiple_of((2 * (z ^ k) + side) * width, width)
            cot_t[pl.ds(start, width), :] = piece.T
    gg_ref[...] = jnp.dot(w_ref[...], cot_t[...], preferred_element_type=F32)
    for half, fg_ref in enumerate((fg0_ref, fg1_ref)):
        cols = half_cols(half)
        fg_ref[...] = (gg_ref[:, cols] * q_ref[:, cols].astype(F32)).astype(BF)


def taps_kernel(scale, turn, place_ref, fg0_ref, fg_ref, fliph, flip0, flip1, *rest):
    *before_ref, taps_ref = rest
    mine = place_ref[3] == turn

    @pl.when(mine)
    def _():
        sum_taps(scale, fg0_ref, fg_ref, fliph, flip0, flip1, taps_ref)

    @pl.when(jnp.logical_not(mine))
    def _():
        taps_ref[...] = before_ref[0][...] if before_ref else jnp.zeros_like(taps_ref)


def sum_taps(scale, fg0_ref, fg_ref, fliph, flip0, flip1, taps_ref):
    for g in range(taps_ref.shape[0]):
        rows = slice(g * GS, (g + 1) * GS)
        mid = flip0[rows, :]
        grads = jnp.concatenate([fg0_ref[rows, :], fg_ref[rows, :]], axis=0)
        window = jnp.concatenate(
            [
                jnp.concatenate([mid, fliph[rows, :]], axis=1),
                jnp.concatenate([flip1[rows, :], mid], axis=1),
            ],
            axis=0,
        )
        moments = lax.dot_general(
            grads, window, (((0,), (0,)), ((), ())), preferred_element_type=F32
        )
        sheared = pltpu.roll(moments, 1, 1, stride=1, stride_axis=0)
        taps_ref[g : g + 1, :] = jnp.sum(sheared[:, FL:], axis=0, keepdims=True) * scale


def backward_kernel(
    fg0_ref, fg1_ref, next_ref, taps_ref, k_ref, v_ref, gg_ref, fil0_ref, fil1_ref, kg_ref, vg_ref, qg_ref
):
    row = lax.broadcasted_iota(jnp.int32, (FL, 2 * FL), 0)
    col = lax.broadcasted_iota(jnp.int32, (FL, 2 * FL), 1)
    wrap = ((row + col) % (2 * FL) == 0).astype(BF)
    back = jnp.dot(taps_ref[...], wrap, preferred_element_type=F32)
    qg_ref[:, :FL] = (gg_ref[:, :FL] * fil0_ref[...].astype(F32)).astype(BF)
    qg_ref[:, FL:] = (gg_ref[:, FL:] * fil1_ref[...].astype(F32)).astype(BF)
    for g in range(taps_ref.shape[0]):
        rows = slice(g * GS, (g + 1) * GS)
        bwd = shear(back[g : g + 1]).astype(BF)
        band = jnp.concatenate([bwd[:, :FL], bwd[:, FL:]], axis=0)
        fg1 = fg1_ref[rows, :]
        window = jnp.concatenate(
            [
                jnp.concatenate([fg0_ref[rows, :], fg1], axis=1),
                jnp.concatenate([fg1, next_ref[rows, :]], axis=1),
            ],
            axis=0,
        )
        both = jnp.dot(window, band, preferred_element_type=F32).astype(BF).astype(F32)
        pg = jnp.concatenate([both[:GS], both[GS:]], axis=1)
        kg_ref[rows, :] = (pg * v_ref[rows, :].astype(F32)).astype(BF)
        vg_ref[rows, :] = (pg * k_ref[rows, :].astype(F32)).astype(BF)


def wave(*values):
    return lax.optimization_barrier(values)


def shift_pairs(n_ctx, n_ten, by):
    ys, halves = 4, 2
    zs = n_ten // 2
    at = lambda x, z, y, core: ((x * halves + z // zs) * ys + y) * n_ten + (z % zs) * 2 + core
    direct, first, second = [], [], []
    for i in range(n_ctx):
        j = i + by
        if not 0 <= j < n_ctx:
            continue
        for t in range(n_ten):
            source, target = i * n_ten + t, j * n_ten + t
            direct.append((source, target))
            if i // ys == j // ys:
                first.append((source, target))
            else:
                relay = at(i // (ys * halves), (i // ys % halves) * zs + t // 2, j % ys, t % 2)
                first.append((source, relay))
                second.append((relay, target))
    return direct, first, second


def body(q_proj, k_proj, v_proj, filter_taps, out_weight, cotangent):
    chans, toks = q_proj.shape
    groups = filter_taps.shape[0]
    feats = out_weight.shape[1]
    width = cotangent.shape[1]
    n_ctx, n_ten = lax.axis_size("context"), lax.axis_size("tensor")
    scale = 1.0 / math.sqrt(GS * toks * n_ctx)
    zs = n_ten // 2
    me = lax.axis_index("tensor")
    place = jnp.stack([me // 2, me % 2, lax.axis_index("context") % 4 == 0, lax.axis_index("context") % 4 == 3]).astype(jnp.int32)
    half_shape = shape(chans, FL)
    gg_shape = shape(chans, toks, dt=F32)

    def move(name, array, axis, pairs):
        with jax.named_scope(name):
            return lax.ppermute(array, axis, pairs)

    def swap(name, array):
        return move(name, array, "tensor", [(j, j ^ 1) for j in range(n_ten)])

    def exchange(name, array, k):
        return move(f"{name}{k}", array, "tensor", [(j, j ^ (2 * k)) for j in range(n_ten)])

    def taps_phase(part, steps):
        got = [move(f"taps_{s}", part, "context", [(i, i ^ s) for i in range(n_ctx)]) for s in steps]
        if len(got) == 1:
            return part + got[0]
        return (part + got[0]) + (got[1] + got[2])

    got = [exchange("cot", cotangent, k) for k in range(1, zs)]
    p1, p0 = [
        (k_proj[:, c].astype(F32) * v_proj[:, c].astype(F32)).astype(BF) for c in map(half_cols, (1, 0))
    ]
    axes = ("context", "tensor")
    direct_pairs, first, second = shift_pairs(n_ctx, n_ten, 1)
    cut = chans // 2
    near = move("halo_near", p1[:cut], axes, first)
    out_half = shape(zs, FL, width)
    scratch = [pltpu.VMEM((FL, chans), BF), pltpu.VMEM((groups, 2 * FL, FL), BF)]
    fil1, mine1, other1, flip0, flip1 = call(
        filter_kernel,
        [half_shape, out_half, out_half, half_shape, half_shape],
        (place, p0, p1, filter_taps, q_proj, out_weight),
        specs=[SM] + [VM] * 5,
        scratch=scratch,
        name="forward1",
    )
    direct = move("halo_direct", p1[cut:], axes, direct_pairs)
    far = move("halo_far", near, axes, second)
    *got, direct, far, other1 = wave(*got, direct, far, other1)

    mate = swap("cot_swap", jnp.stack([cotangent, *got]))
    there1 = swap("out1_swap", other1)
    fil0, mine0, other0, fliph = call(
        filter_first_kernel,
        [half_shape, out_half, out_half, half_shape],
        (place, near, far, direct, p0, filter_taps, q_proj, out_weight),
        specs=[SM] + [VM] * 7,
        scratch=scratch + [pltpu.VMEM((chans, FL), BF)],
        name="forward0",
    )
    there0 = swap("out0_swap", other0)
    mate, fil0 = wave(mate, fil0)
    gg, fg0, fg1 = call(
        grad_kernel,
        [gg_shape, half_shape, half_shape],
        (place, cotangent, *got, mate, out_weight, q_proj),
        specs=[SM] + [VM] * (zs + 3),
        scratch=[pltpu.VMEM((feats, toks), BF)],
        name="grad",
    )
    near, fg1 = wave(near, fg1)
    def taps(turn, *before):
        return call(
            lambda *refs: taps_kernel(scale, turn, *refs),
            [shape(groups, FL, dt=F32)],
            (place, fg0, fg1, fliph, flip0, flip1, *before),
            specs=[SM] + [VM] * (5 + len(before)),
            name=f"taps{turn}",
        )[0]

    taps_part = taps(0)
    fg0_sent, taps_part = wave(fg0, taps_part)
    after = move("after", fg0_sent, "context", [(i + 1, i) for i in range(n_ctx - 1)])
    taps_part = taps(1, taps_part)
    total = jnp.concatenate(
        [m.astype(F32) + t.astype(F32) for m, t in ((mine0, there0), (mine1, there1))], axis=1
    )
    rest = [exchange("out", total[k].astype(BF), k) for k in range(1, zs)]
    taps_part = taps_phase(taps_part, [8])
    taps_part = taps_phase(taps_part, [16])
    taps_part = taps_phase(taps_part, [1])
    taps_part = taps_phase(taps_part, [2])
    after, *rest = wave(after, *rest)
    k_grad, v_grad, q_grad = call(
        backward_kernel,
        [shape(chans, toks)] * 3,
        (fg0, fg1, after, filter_taps, k_proj, v_proj, gg, fil0, fil1),
        name="backward",
    )
    last = move("taps_4", taps_part, "context", [(i, i ^ 4) for i in range(n_ctx)])
    block_output = total[0]
    for part in rest:
        block_output = block_output + part.astype(F32)
    block_output = block_output.astype(BF)
    last, k_grad, block_output = wave(last, k_grad, block_output)
    taps_part = taps_part + last
    return (block_output, q_grad, k_grad, v_grad, taps_part)


def solution(mesh):
    placed = (
        P("tensor", "context"),
        P("tensor", "context"),
        P("tensor", "context"),
        P("tensor", None),
        P("tensor", None),
        P("context", "tensor"),
    )
    return jax.shard_map(
        body,
        mesh=mesh,
        in_specs=placed,
        out_specs=(
            P("context", "tensor"),
            P("tensor", "context"),
            P("tensor", "context"),
            P("tensor", "context"),
            P("tensor", None),
        ),
        check_vma=False,
    )
```

```python
import math

import jax
import jax.numpy as jnp
from jax import lax
from jax.experimental import pallas as pl
from jax.experimental.pallas import tpu as pltpu
from jax.sharding import PartitionSpec as P

D = 8192
GROUPS = 512
FL = 128
GS = D // GROUPS
F32 = jnp.float32
BF = jnp.bfloat16
VM = pl.BlockSpec(memory_space=pltpu.VMEM)
SM = pl.BlockSpec(memory_space=pltpu.SMEM)
PARAMS = pltpu.CompilerParams(vmem_limit_bytes=16 << 20)


def call(kernel, outs, args, specs=None, out_specs=None, scratch=(), name=None, aliases=None):
    return pl.pallas_call(
        kernel,
        out_shape=outs,
        in_specs=[VM] * len(args) if specs is None else specs,
        out_specs=[VM] * len(outs) if out_specs is None else out_specs,
        scratch_shapes=list(scratch),
        compiler_params=PARAMS,
        input_output_aliases=aliases or {},
        cost_estimate=pl.CostEstimate(flops=1, bytes_accessed=1, transcendentals=0),
        name=name,
    )(*args)


def shape(*dims, dt=BF):
    return jax.ShapeDtypeStruct(dims, dt)


def shear(row):
    return pltpu.roll(jnp.broadcast_to(row, (FL, 2 * FL)), 0, 1, stride=1, stride_axis=0)


def flip(array):
    row = lax.broadcasted_iota(jnp.int32, (FL, FL), 0)
    col = lax.broadcasted_iota(jnp.int32, (FL, FL), 1)
    return jnp.dot(array, (row + col == FL - 1).astype(BF), preferred_element_type=F32).astype(BF)


def half_cols(half):
    return slice(half * FL, (half + 1) * FL)


def forward_bands(taps_ref, band):
    taps = taps_ref[...].astype(F32)
    ahead = jnp.concatenate([taps, jnp.zeros_like(taps)], axis=1)
    for g in range(taps.shape[0]):
        fwd = shear(ahead[g : g + 1]).astype(BF)
        band[g, :FL, :] = fwd[:, FL:]
        band[g, FL:, :] = fwd[:, :FL]


def run_filter(prev_ref, cur_ref, band, fil_ref):
    for g in range(band.shape[0]):
        rows = slice(g * GS, (g + 1) * GS)
        window = jnp.concatenate([prev_ref[rows, :], cur_ref[rows, :]], axis=1)
        fil_ref[rows, :] = jnp.dot(window, band[g], preferred_element_type=F32).astype(BF)


def filter_kernel(place_ref, p0_ref, p1_ref, taps_ref, q_ref, w_ref, fil_ref, mine_ref, other_ref, flip0_ref, flip1_ref, gated_t, band):
    forward_bands(taps_ref, band)
    flip0_ref[...] = flip(p0_ref[...])
    flip1_ref[...] = flip(p1_ref[...])
    run_filter(p0_ref, p1_ref, band, fil_ref)
    project(1, place_ref, q_ref, fil_ref, w_ref, mine_ref, other_ref, gated_t)


def project(half, place_ref, q_ref, fil_ref, w_ref, mine_ref, other_ref, gated_t):
    gated_t[...] = (q_ref[:, half_cols(half)].astype(F32) * fil_ref[...].astype(F32)).astype(BF).T
    z, core = place_ref[0], place_ref[1]
    chips, _, width = mine_ref.shape
    for k in range(chips):
        for ref, side in ((other_ref, 1 - core), (mine_ref, core)):
            start = pl.multiple_of((2 * (z ^ k) + side) * width, width)
            ref[k] = jnp.dot(
                gated_t[...], w_ref[:, pl.ds(start, width)], preferred_element_type=F32
            ).astype(BF)


def filter_first_kernel(
    place_ref, near_ref, far_ref, direct_ref, p0_ref, taps_ref, q_ref, w_ref,
    fil_ref, mine_ref, other_ref, flip_ref, gated_t, band, halo,
):
    cut = near_ref.shape[0]
    halo[:cut, :] = jnp.where(place_ref[2] == 1, far_ref[...], near_ref[...])
    halo[cut:, :] = direct_ref[...]
    forward_bands(taps_ref, band)
    flip_ref[...] = flip(halo[...])
    run_filter(halo, p0_ref, band, fil_ref)
    project(0, place_ref, q_ref, fil_ref, w_ref, mine_ref, other_ref, gated_t)


def grad_kernel(place_ref, own_ref, g1, g2, g3, mate_ref, w_ref, q_ref, gg_ref, fg0_ref, fg1_ref, cot_t):
    z, core = place_ref[0], place_ref[1]
    width = own_ref.shape[1]
    for k, got in enumerate((own_ref, g1, g2, g3)):
        for piece, side in ((got[...], core), (mate_ref[k], 1 - core)):
            start = pl.multiple_of((2 * (z ^ k) + side) * width, width)
            cot_t[pl.ds(start, width), :] = piece.T
    gg_ref[...] = jnp.dot(w_ref[...], cot_t[...], preferred_element_type=F32)
    for half, fg_ref in enumerate((fg0_ref, fg1_ref)):
        cols = half_cols(half)
        fg_ref[...] = (gg_ref[:, cols] * q_ref[:, cols].astype(F32)).astype(BF)


def taps_kernel(scale, turn, place_ref, fg0_ref, fg_ref, fliph, flip0, flip1, *rest):
    *before_ref, taps_ref = rest
    mine = place_ref[3] == turn

    @pl.when(mine)
    def _():
        sum_taps(scale, fg0_ref, fg_ref, fliph, flip0, flip1, taps_ref)

    if not before_ref:

        @pl.when(jnp.logical_not(mine))
        def _():
            taps_ref[...] = jnp.zeros_like(taps_ref)


def sum_taps(scale, fg0_ref, fg_ref, fliph, flip0, flip1, taps_ref):
    for g in range(taps_ref.shape[0]):
        rows = slice(g * GS, (g + 1) * GS)
        mid = flip0[rows, :]
        grads = jnp.concatenate([fg0_ref[rows, :], fg_ref[rows, :]], axis=0)
        window = jnp.concatenate(
            [
                jnp.concatenate([mid, fliph[rows, :]], axis=1),
                jnp.concatenate([flip1[rows, :], mid], axis=1),
            ],
            axis=0,
        )
        moments = lax.dot_general(
            grads, window, (((0,), (0,)), ((), ())), preferred_element_type=F32
        )
        sheared = pltpu.roll(moments, 1, 1, stride=1, stride_axis=0)
        taps_ref[g : g + 1, :] = jnp.sum(sheared[:, FL:], axis=0, keepdims=True) * scale


def backward_kernel(
    fg0_ref, fg1_ref, next_ref, taps_ref, k_ref, v_ref, gg_ref, fil0_ref, fil1_ref, kg_ref, vg_ref, qg_ref
):
    row = lax.broadcasted_iota(jnp.int32, (FL, 2 * FL), 0)
    col = lax.broadcasted_iota(jnp.int32, (FL, 2 * FL), 1)
    wrap = ((row + col) % (2 * FL) == 0).astype(BF)
    back = jnp.dot(taps_ref[...], wrap, preferred_element_type=F32)
    qg_ref[:, :FL] = (gg_ref[:, :FL] * fil0_ref[...].astype(F32)).astype(BF)
    qg_ref[:, FL:] = (gg_ref[:, FL:] * fil1_ref[...].astype(F32)).astype(BF)
    for g in range(taps_ref.shape[0]):
        rows = slice(g * GS, (g + 1) * GS)
        bwd = shear(back[g : g + 1]).astype(BF)
        band = jnp.concatenate([bwd[:, :FL], bwd[:, FL:]], axis=0)
        fg1 = fg1_ref[rows, :]
        window = jnp.concatenate(
            [
                jnp.concatenate([fg0_ref[rows, :], fg1], axis=1),
                jnp.concatenate([fg1, next_ref[rows, :]], axis=1),
            ],
            axis=0,
        )
        both = jnp.dot(window, band, preferred_element_type=F32).astype(BF).astype(F32)
        pg = jnp.concatenate([both[:GS], both[GS:]], axis=1)
        kg_ref[rows, :] = (pg * v_ref[rows, :].astype(F32)).astype(BF)
        vg_ref[rows, :] = (pg * k_ref[rows, :].astype(F32)).astype(BF)


def wave(*values):
    return lax.optimization_barrier(values)


def shift_pairs(n_ctx, n_ten, by):
    ys, halves = 4, 2
    zs = n_ten // 2
    at = lambda x, z, y, core: ((x * halves + z // zs) * ys + y) * n_ten + (z % zs) * 2 + core
    direct, first, second = [], [], []
    for i in range(n_ctx):
        j = i + by
        if not 0 <= j < n_ctx:
            continue
        for t in range(n_ten):
            source, target = i * n_ten + t, j * n_ten + t
            direct.append((source, target))
            if i // ys == j // ys:
                first.append((source, target))
            else:
                relay = at(i // (ys * halves), (i // ys % halves) * zs + t // 2, j % ys, t % 2)
                first.append((source, relay))
                second.append((relay, target))
    return direct, first, second


def body(q_proj, k_proj, v_proj, filter_taps, out_weight, cotangent):
    chans, toks = q_proj.shape
    groups = filter_taps.shape[0]
    feats = out_weight.shape[1]
    width = cotangent.shape[1]
    n_ctx, n_ten = lax.axis_size("context"), lax.axis_size("tensor")
    scale = 1.0 / math.sqrt(GS * toks * n_ctx)
    zs = n_ten // 2
    me = lax.axis_index("tensor")
    place = jnp.stack([me // 2, me % 2, lax.axis_index("context") % 4 == 0, lax.axis_index("context") % 4 == 3]).astype(jnp.int32)
    half_shape = shape(chans, FL)
    gg_shape = shape(chans, toks, dt=F32)

    def move(name, array, axis, pairs):
        with jax.named_scope(name):
            return lax.ppermute(array, axis, pairs)

    def swap(name, array):
        return move(name, array, "tensor", [(j, j ^ 1) for j in range(n_ten)])

    def exchange(name, array, k):
        return move(f"{name}{k}", array, "tensor", [(j, j ^ (2 * k)) for j in range(n_ten)])

    def taps_phase(part, steps):
        got = [move(f"taps_{s}", part, "context", [(i, i ^ s) for i in range(n_ctx)]) for s in steps]
        if len(got) == 1:
            return part + got[0]
        return (part + got[0]) + (got[1] + got[2])

    got = [exchange("cot", cotangent, k) for k in range(1, zs)]
    p1, p0 = [
        (k_proj[:, c].astype(F32) * v_proj[:, c].astype(F32)).astype(BF) for c in map(half_cols, (1, 0))
    ]
    axes = ("context", "tensor")
    direct_pairs, first, second = shift_pairs(n_ctx, n_ten, 1)
    cut = chans // 2
    near = move("halo_near", p1[:cut], axes, first)
    out_half = shape(zs, FL, width)
    scratch = [pltpu.VMEM((FL, chans), BF), pltpu.VMEM((groups, 2 * FL, FL), BF)]
    fil1, mine1, other1, flip0, flip1 = call(
        filter_kernel,
        [half_shape, out_half, out_half, half_shape, half_shape],
        (place, p0, p1, filter_taps, q_proj, out_weight),
        specs=[SM] + [VM] * 5,
        scratch=scratch,
        name="forward1",
    )
    direct = move("halo_direct", p1[cut:], axes, direct_pairs)
    far = move("halo_far", near, axes, second)
    *got, direct, far, other1 = wave(*got, direct, far, other1)

    mate = swap("cot_swap", jnp.stack([cotangent, *got]))
    there1 = swap("out1_swap", other1)
    fil0, mine0, other0, fliph = call(
        filter_first_kernel,
        [half_shape, out_half, out_half, half_shape],
        (place, near, far, direct, p0, filter_taps, q_proj, out_weight),
        specs=[SM] + [VM] * 7,
        scratch=scratch + [pltpu.VMEM((chans, FL), BF)],
        name="forward0",
    )
    there0 = swap("out0_swap", other0)
    mate, fil0 = wave(mate, fil0)
    gg, fg0, fg1 = call(
        grad_kernel,
        [gg_shape, half_shape, half_shape],
        (place, cotangent, *got, mate, out_weight, q_proj),
        specs=[SM] + [VM] * (zs + 3),
        scratch=[pltpu.VMEM((feats, toks), BF)],
        name="grad",
    )
    near, fg1 = wave(near, fg1)
    def taps(turn, *before):
        return call(
            lambda *refs: taps_kernel(scale, turn, *refs),
            [shape(groups, FL, dt=F32)],
            (place, fg0, fg1, fliph, flip0, flip1, *before),
            specs=[SM] + [VM] * (5 + len(before)),
            name=f"taps{turn}",
            aliases={6: 0} if before else None,
        )[0]

    taps_part = taps(0)
    fg0_sent, _ = wave(fg0, taps_part)
    after = move("after", fg0_sent, "context", [(i + 1, i) for i in range(n_ctx - 1)])
    taps_part = taps(1, taps_part)
    total = jnp.concatenate(
        [m.astype(F32) + t.astype(F32) for m, t in ((mine0, there0), (mine1, there1))], axis=1
    )
    rest = [exchange("out", total[k].astype(BF), k) for k in range(1, zs)]
    taps_part = taps_phase(taps_part, [8])
    taps_part = taps_phase(taps_part, [16])
    taps_part = taps_phase(taps_part, [1])
    taps_part = taps_phase(taps_part, [2])
    after, *rest = wave(after, *rest)
    k_grad, v_grad, q_grad = call(
        backward_kernel,
        [shape(chans, toks)] * 3,
        (fg0, fg1, after, filter_taps, k_proj, v_proj, gg, fil0, fil1),
        name="backward",
    )
    last = move("taps_4", taps_part, "context", [(i, i ^ 4) for i in range(n_ctx)])
    block_output = total[0]
    for part in rest:
        block_output = block_output + part.astype(F32)
    block_output = block_output.astype(BF)
    last, k_grad, block_output = wave(last, k_grad, block_output)
    taps_part = taps_part + last
    return (block_output, q_grad, k_grad, v_grad, taps_part)


def solution(mesh):
    placed = (
        P("tensor", "context"),
        P("tensor", "context"),
        P("tensor", "context"),
        P("tensor", None),
        P("tensor", None),
        P("context", "tensor"),
    )
    return jax.shard_map(
        body,
        mesh=mesh,
        in_specs=placed,
        out_specs=(
            P("context", "tensor"),
            P("tensor", "context"),
            P("tensor", "context"),
            P("tensor", "context"),
            P("tensor", None),
        ),
        check_vma=False,
    )
```

```python
import math

import jax
import jax.numpy as jnp
from jax import lax
from jax.experimental import pallas as pl
from jax.experimental.pallas import tpu as pltpu
from jax.sharding import PartitionSpec as P

D = 8192
GROUPS = 512
FL = 128
GS = D // GROUPS
F32 = jnp.float32
BF = jnp.bfloat16
VM = pl.BlockSpec(memory_space=pltpu.VMEM)
SM = pl.BlockSpec(memory_space=pltpu.SMEM)
PARAMS = pltpu.CompilerParams(vmem_limit_bytes=16 << 20)


def call(kernel, outs, args, specs=None, out_specs=None, scratch=(), name=None, aliases=None):
    return pl.pallas_call(
        kernel,
        out_shape=outs,
        in_specs=[VM] * len(args) if specs is None else specs,
        out_specs=[VM] * len(outs) if out_specs is None else out_specs,
        scratch_shapes=list(scratch),
        compiler_params=PARAMS,
        input_output_aliases=aliases or {},
        cost_estimate=pl.CostEstimate(flops=1, bytes_accessed=1, transcendentals=0),
        name=name,
    )(*args)


def shape(*dims, dt=BF):
    return jax.ShapeDtypeStruct(dims, dt)


def shear(row):
    return pltpu.roll(jnp.broadcast_to(row, (FL, 2 * FL)), 0, 1, stride=1, stride_axis=0)


def flip(array):
    row = lax.broadcasted_iota(jnp.int32, (FL, FL), 0)
    col = lax.broadcasted_iota(jnp.int32, (FL, FL), 1)
    return jnp.dot(array, (row + col == FL - 1).astype(BF), preferred_element_type=F32).astype(BF)


def half_cols(half):
    return slice(half * FL, (half + 1) * FL)


def forward_bands(taps_ref, band):
    taps = taps_ref[...].astype(F32)
    ahead = jnp.concatenate([taps, jnp.zeros_like(taps)], axis=1)
    for g in range(taps.shape[0]):
        fwd = shear(ahead[g : g + 1]).astype(BF)
        band[g, :FL, :] = fwd[:, FL:]
        band[g, FL:, :] = fwd[:, :FL]


def run_filter(prev_ref, cur_ref, band, fil_ref):
    for g in range(band.shape[0]):
        rows = slice(g * GS, (g + 1) * GS)
        window = jnp.concatenate([prev_ref[rows, :], cur_ref[rows, :]], axis=1)
        fil_ref[rows, :] = jnp.dot(window, band[g], preferred_element_type=F32).astype(BF)


def filter_kernel(place_ref, p0_ref, p1_ref, taps_ref, q_ref, w_ref, fil_ref, mine_ref, other_ref, flip0_ref, flip1_ref, gated_t, band):
    forward_bands(taps_ref, band)
    flip0_ref[...] = flip(p0_ref[...])
    flip1_ref[...] = flip(p1_ref[...])
    run_filter(p0_ref, p1_ref, band, fil_ref)
    project(1, place_ref, q_ref, fil_ref, w_ref, mine_ref, other_ref, gated_t)


def project(half, place_ref, q_ref, fil_ref, w_ref, mine_ref, other_ref, gated_t):
    gated_t[...] = (q_ref[:, half_cols(half)].astype(F32) * fil_ref[...].astype(F32)).astype(BF).T
    z, core = place_ref[0], place_ref[1]
    chips, _, width = mine_ref.shape
    for k in range(chips):
        for ref, side in ((other_ref, 1 - core), (mine_ref, core)):
            start = pl.multiple_of((2 * (z ^ k) + side) * width, width)
            ref[k] = jnp.dot(
                gated_t[...], w_ref[:, pl.ds(start, width)], preferred_element_type=F32
            ).astype(BF)


def filter_first_kernel(
    place_ref, near_ref, far_ref, direct_ref, p0_ref, taps_ref, q_ref, w_ref,
    fil_ref, mine_ref, other_ref, flip_ref, gated_t, band, halo,
):
    cut = near_ref.shape[0]
    halo[:cut, :] = jnp.where(place_ref[2] == 1, far_ref[...], near_ref[...])
    halo[cut:, :] = direct_ref[...]
    forward_bands(taps_ref, band)
    flip_ref[...] = flip(halo[...])
    run_filter(halo, p0_ref, band, fil_ref)
    project(0, place_ref, q_ref, fil_ref, w_ref, mine_ref, other_ref, gated_t)


def grad_kernel(place_ref, own_ref, g1, g2, g3, mate_ref, w_ref, q_ref, gg_ref, fg0_ref, fg1_ref, cot_t):
    z, core = place_ref[0], place_ref[1]
    width = own_ref.shape[1]
    for k, got in enumerate((own_ref, g1, g2, g3)):
        for piece, side in ((got[...], core), (mate_ref[k], 1 - core)):
            start = pl.multiple_of((2 * (z ^ k) + side) * width, width)
            cot_t[pl.ds(start, width), :] = piece.T
    gg_ref[...] = jnp.dot(w_ref[...], cot_t[...], preferred_element_type=F32)
    for half, fg_ref in enumerate((fg0_ref, fg1_ref)):
        cols = half_cols(half)
        fg_ref[...] = (gg_ref[:, cols] * q_ref[:, cols].astype(F32)).astype(BF)


def taps_kernel(scale, turn, place_ref, fg0_ref, fg_ref, fliph, flip0, flip1, *rest):
    *before_ref, taps_ref = rest
    mine = place_ref[3] == turn

    @pl.when(mine)
    def _():
        sum_taps(scale, fg0_ref, fg_ref, fliph, flip0, flip1, taps_ref)

    if not before_ref:

        @pl.when(jnp.logical_not(mine))
        def _():
            taps_ref[...] = jnp.zeros_like(taps_ref)


def sum_taps(scale, fg0_ref, fg_ref, fliph, flip0, flip1, taps_ref):
    for g in range(taps_ref.shape[0]):
        rows = slice(g * GS, (g + 1) * GS)
        mid = flip0[rows, :]
        grads = jnp.concatenate([fg0_ref[rows, :], fg_ref[rows, :]], axis=0)
        window = jnp.concatenate(
            [
                jnp.concatenate([mid, fliph[rows, :]], axis=1),
                jnp.concatenate([flip1[rows, :], mid], axis=1),
            ],
            axis=0,
        )
        moments = lax.dot_general(
            grads, window, (((0,), (0,)), ((), ())), preferred_element_type=F32
        )
        sheared = pltpu.roll(moments, 1, 1, stride=1, stride_axis=0)
        taps_ref[g : g + 1, :] = jnp.sum(sheared[:, FL:], axis=0, keepdims=True) * scale


def backward_kernel(
    fg0_ref, fg1_ref, next_ref, taps_ref, k_ref, v_ref, gg_ref, fil0_ref, fil1_ref, kg_ref, vg_ref, qg_ref
):
    row = lax.broadcasted_iota(jnp.int32, (FL, 2 * FL), 0)
    col = lax.broadcasted_iota(jnp.int32, (FL, 2 * FL), 1)
    wrap = ((row + col) % (2 * FL) == 0).astype(BF)
    back = jnp.dot(taps_ref[...], wrap, preferred_element_type=F32)
    qg_ref[:, :FL] = (gg_ref[:, :FL] * fil0_ref[...].astype(F32)).astype(BF)
    qg_ref[:, FL:] = (gg_ref[:, FL:] * fil1_ref[...].astype(F32)).astype(BF)
    for g in range(taps_ref.shape[0]):
        rows = slice(g * GS, (g + 1) * GS)
        bwd = shear(back[g : g + 1]).astype(BF)
        band = jnp.concatenate([bwd[:, :FL], bwd[:, FL:]], axis=0)
        fg1 = fg1_ref[rows, :]
        window = jnp.concatenate(
            [
                jnp.concatenate([fg0_ref[rows, :], fg1], axis=1),
                jnp.concatenate([fg1, next_ref[rows, :]], axis=1),
            ],
            axis=0,
        )
        both = jnp.dot(window, band, preferred_element_type=F32).astype(BF).astype(F32)
        pg = jnp.concatenate([both[:GS], both[GS:]], axis=1)
        kg_ref[rows, :] = (pg * v_ref[rows, :].astype(F32)).astype(BF)
        vg_ref[rows, :] = (pg * k_ref[rows, :].astype(F32)).astype(BF)


def wave(*values):
    return lax.optimization_barrier(values)


def shift_pairs(n_ctx, n_ten, by):
    ys, halves = 4, 2
    zs = n_ten // 2
    at = lambda x, z, y, core: ((x * halves + z // zs) * ys + y) * n_ten + (z % zs) * 2 + core
    direct, first, second = [], [], []
    for i in range(n_ctx):
        j = i + by
        if not 0 <= j < n_ctx:
            continue
        for t in range(n_ten):
            source, target = i * n_ten + t, j * n_ten + t
            direct.append((source, target))
            if i // ys == j // ys:
                first.append((source, target))
            else:
                relay = at(i // (ys * halves), (i // ys % halves) * zs + t // 2, j % ys, t % 2)
                first.append((source, relay))
                second.append((relay, target))
    return direct, first, second


def body(q_proj, k_proj, v_proj, filter_taps, out_weight, cotangent):
    chans, toks = q_proj.shape
    groups = filter_taps.shape[0]
    feats = out_weight.shape[1]
    width = cotangent.shape[1]
    n_ctx, n_ten = lax.axis_size("context"), lax.axis_size("tensor")
    scale = 1.0 / math.sqrt(GS * toks * n_ctx)
    zs = n_ten // 2
    me = lax.axis_index("tensor")
    place = jnp.stack([me // 2, me % 2, lax.axis_index("context") % 4 == 0, lax.axis_index("context") % 4 == 3]).astype(jnp.int32)
    half_shape = shape(chans, FL)
    gg_shape = shape(chans, toks, dt=F32)

    def move(name, array, axis, pairs):
        with jax.named_scope(name):
            return lax.ppermute(array, axis, pairs)

    def swap(name, array):
        return move(name, array, "tensor", [(j, j ^ 1) for j in range(n_ten)])

    def exchange(name, array, k):
        return move(f"{name}{k}", array, "tensor", [(j, j ^ (2 * k)) for j in range(n_ten)])

    def taps_phase(part, steps):
        got = [move(f"taps_{s}", part, "context", [(i, i ^ s) for i in range(n_ctx)]) for s in steps]
        if len(got) == 1:
            return part + got[0]
        return (part + got[0]) + (got[1] + got[2])

    got = [exchange("cot", cotangent, k) for k in range(1, zs)]
    p1, p0 = [
        (k_proj[:, c].astype(F32) * v_proj[:, c].astype(F32)).astype(BF) for c in map(half_cols, (1, 0))
    ]
    axes = ("context", "tensor")
    direct_pairs, first, second = shift_pairs(n_ctx, n_ten, 1)
    cut = chans // 2
    near = move("halo_near", p1[:cut], axes, first)
    out_half = shape(zs, FL, width)
    scratch = [pltpu.VMEM((FL, chans), BF), pltpu.VMEM((groups, 2 * FL, FL), BF)]
    fil1, mine1, other1, flip0, flip1 = call(
        filter_kernel,
        [half_shape, out_half, out_half, half_shape, half_shape],
        (place, p0, p1, filter_taps, q_proj, out_weight),
        specs=[SM] + [VM] * 5,
        scratch=scratch,
        name="forward1",
    )
    direct = move("halo_direct", p1[cut:], axes, direct_pairs)
    far = move("halo_far", near, axes, second)
    *got, direct, far, other1 = wave(*got, direct, far, other1)

    mate = swap("cot_swap", jnp.stack([cotangent, *got]))
    there1 = swap("out1_swap", other1)
    fil0, mine0, other0, fliph = call(
        filter_first_kernel,
        [half_shape, out_half, out_half, half_shape],
        (place, near, far, direct, p0, filter_taps, q_proj, out_weight),
        specs=[SM] + [VM] * 7,
        scratch=scratch + [pltpu.VMEM((chans, FL), BF)],
        name="forward0",
    )
    there0 = swap("out0_swap", other0)
    mate, fil0 = wave(mate, fil0)
    gg, fg0, fg1 = call(
        grad_kernel,
        [gg_shape, half_shape, half_shape],
        (place, cotangent, *got, mate, out_weight, q_proj),
        specs=[SM] + [VM] * (zs + 3),
        scratch=[pltpu.VMEM((feats, toks), BF)],
        name="grad",
    )
    near, fg1 = wave(near, fg1)
    def taps(turn, *before):
        return call(
            lambda *refs: taps_kernel(scale, turn, *refs),
            [shape(groups, FL, dt=F32)],
            (place, fg0, fg1, fliph, flip0, flip1, *before),
            specs=[SM] + [VM] * (5 + len(before)),
            name=f"taps{turn}",
            aliases={6: 0} if before else None,
        )[0]

    taps_part = taps(0)
    fg0_sent, _ = wave(fg0, taps_part)
    after = move("after", fg0_sent, "context", [(i + 1, i) for i in range(n_ctx - 1)])
    taps_part = taps(1, taps_part)
    total = jnp.concatenate(
        [m.astype(F32) + t.astype(F32) for m, t in ((mine0, there0), (mine1, there1))], axis=1
    )
    rest = [exchange("out", total[k].astype(BF), k) for k in range(1, zs)]
    taps_part = taps_phase(taps_part, [8])
    taps_part = taps_phase(taps_part, [16])
    taps_part = taps_phase(taps_part, [2])
    taps_part = taps_phase(taps_part, [1])
    after, *rest = wave(after, *rest)
    k_grad, v_grad, q_grad = call(
        backward_kernel,
        [shape(chans, toks)] * 3,
        (fg0, fg1, after, filter_taps, k_proj, v_proj, gg, fil0, fil1),
        name="backward",
    )
    last = move("taps_4", taps_part, "context", [(i, i ^ 4) for i in range(n_ctx)])
    block_output = total[0]
    for part in rest:
        block_output = block_output + part.astype(F32)
    block_output = block_output.astype(BF)
    last, k_grad, block_output = wave(last, k_grad, block_output)
    taps_part = taps_part + last
    return (block_output, q_grad, k_grad, v_grad, taps_part)


def solution(mesh):
    placed = (
        P("tensor", "context"),
        P("tensor", "context"),
        P("tensor", "context"),
        P("tensor", None),
        P("tensor", None),
        P("context", "tensor"),
    )
    return jax.shard_map(
        body,
        mesh=mesh,
        in_specs=placed,
        out_specs=(
            P("context", "tensor"),
            P("tensor", "context"),
            P("tensor", "context"),
            P("tensor", "context"),
            P("tensor", None),
        ),
        check_vma=False,
    )
```
